32 devices in a mesh: groups: 2 (over y), frames: 4 (over z), heads: 2 (over x), rep: 2 (over core).
Axes of the slice: x: 2, y: 2, z: 4, core: 2. Of those that a mesh axis runs over, the one named last changes fastest.
Arguments:
- query: bfloat16 [4096, 3072], P(('groups', 'frames', 'rep'), 'heads'), parts along dimension 0, may hold values from -120 to 120
- key_proj: bfloat16 [4096, 3072], P(('groups', 'frames', 'rep'), 'heads'), parts along dimension 0, may hold values from -4 to 4
- value: bfloat16 [4096, 3072], P(('groups', 'frames', 'rep'), 'heads'), parts along dimension 0, may hold values from -6 to 6
- block_mask: int32 [24, 8, 8], P('heads'), may hold values from 0 to 1, as said below
- tile_sizes: int32 [2, 4], P('rep'), may hold values from 1 to 128, 256 in all within a row
- temporal_ids: int32 [8], P('heads'), may hold values from 0 to 23, as said below
Outputs:
- attended: bfloat16 [4096, 3072], P(('groups', 'frames', 'rep'), 'heads'), parts along dimension 0
The draws below stay inside these ranges and needn't reach their ends.
There are 2 independent parts, one for each index of `groups`. The reference program is written for one: setup_inputs(seed, part) draws one part's arguments, and reference() takes and returns one part's arrays. A program takes and returns all parts, laid end to end along the dimension named above; an argument that names none is the same for every part. Nothing has to cross between parts.
Inputs may be any that keep to these rules, and one draw needn't show every extreme that they name: `block_mask`: each row of each head's block mask has exactly 4 ones, its diagonal entry among them. Entries j of temporal_ids are distinct and lie in heads (j // 4) * 12 to (j // 4 + 1) * 12 - 1. `tile_sizes`: each row sums to 256, and its largest entry is 128.
All inputs are finite; a program needn't handle non-finite values.
Results may differ from the reference program's by a relative error of at most 0.008.
Values may be sent and summed in bfloat16 or wider, within the bound.
A program may use at most 64 MiB of HBM per device.

```python
import math
import jax
import jax.numpy as jnp
import numpy as np
from jax import lax

HEADS = 24
HD = 128
TEMP = 8
BLK = 64
HALF = 256
HPD = 12
TPD = 4
WIDTH = 3072
FRAME = 512
NB = 8
LIVE = 4
TILE_MAX = 128
TOKENS = 2048
N_FRAMES = 4
N_REP = 2


def base_keys(key):
    return jnp.clip(jax.random.normal(jax.random.fold_in(key, 7), (TOKENS, WIDTH), jnp.float32), -4.0, 4.0)


def draw_key_proj(key, part):
    keys_drawn = base_keys(key)
    return keys_drawn.astype(jnp.bfloat16)


def draw_query(key, part):
    drawn = jnp.clip(jax.random.normal(jax.random.fold_in(key, 11), (TOKENS, WIDTH), jnp.float32), -4.0, 4.0)
    return drawn.astype(jnp.bfloat16)


def draw_block_mask(key, part):
    ranks_raw = jax.random.randint(key, (HEADS, NB, NB), 0, 1 << 20) * NB + jnp.arange(NB, dtype=jnp.int32)[None, None, :]
    diagonal = jnp.eye(NB, dtype=jnp.int32)[None] == 1
    ranks_raw = jnp.where(diagonal, -1, ranks_raw)
    placing = jnp.argsort(jnp.argsort(ranks_raw, axis=-1), axis=-1)
    return (placing < LIVE).astype(jnp.int32)


def draw_temporal_ids(key, part):
    block_total = TEMP // TPD
    split_keys = jax.random.split(key, block_total)
    picks = jax.vmap(lambda one_key: jax.random.permutation(one_key, HPD)[:TPD])(split_keys)
    offsets = jnp.arange(block_total, dtype=jnp.int32)[:, None] * HPD
    return (picks.astype(jnp.int32) + offsets).reshape(TEMP).astype(jnp.int32)


def levels(stream_key, extent, cuts, low, largest):
    loudness, own = 1.0, jax.random.fold_in(stream_key, 6)
    for dim, blocks in cuts:
        heights = jnp.exp(jax.random.uniform(jax.random.fold_in(own, dim), (blocks,), jnp.float32, low / len(cuts), largest / len(cuts)))
        loudness = loudness * jnp.repeat(heights, extent[dim] // blocks).reshape([-1 if axis == dim else 1 for axis in range(len(extent))])
    return loudness


def length_profile(amount, total, bound, lean):
    loads = [(1 << 20) // math.isqrt(standing ** lean) + 1 for standing in range(2, amount + 1)]
    surplus, counts = total - bound - (amount - 1), [1] * (amount - 1)
    while surplus > 0:
        candidates = [i for i in range(amount - 1) if counts[i] < bound]
        mass, remaining = sum([loads[i] for i in candidates]), surplus
        for i in candidates:
            more = min(bound - counts[i], max(1, remaining * loads[i] // mass), surplus)
            counts[i] = counts[i] + more
            surplus = surplus - more
    return np.array([bound] + counts)


def ragged_sizes(stream_key, amount, total, most, lean):
    if amount == 2:
        one = jax.random.randint(stream_key, (), max(1, total - most), min(most, total - 1) + 1)
        return jnp.stack([one, total - one])
    lengths = jnp.asarray(length_profile(amount, total, most, lean), jnp.int32)
    twos = (amount - 1) // 2
    source_of, receiver = lengths[1:1 + 2 * twos:2], lengths[2:2 + 2 * twos:2]
    room = jnp.minimum(source_of - 1, most - receiver)
    shifted = jax.random.randint(jax.random.fold_in(stream_key, 1), (twos,), 0, 1 << 20) % (room + 1)
    lengths = lengths.at[1:1 + 2 * twos:2].set(source_of - shifted).at[2:2 + 2 * twos:2].set(receiver + shifted)
    return lengths[jax.random.permutation(jax.random.fold_in(stream_key, 2), amount)]


def noise(stream_key, dims, scale, reach, cuts=(), held_as=jnp.bfloat16):
    values = scale * jax.random.normal(stream_key, dims, jnp.float32)
    if cuts:
        values = values * levels(stream_key, dims, cuts, -0.22, 0.18)
    return jnp.clip(values, -reach, reach).astype(held_as)


def setup_inputs(seed: int = 0, part: int = 0) -> dict:
    seeds = jax.random.split(jax.random.key(seed), 7)
    part_splits = jax.random.split(jax.random.fold_in(seeds[6], part), 7)
    query = draw_query(jax.random.fold_in(jax.random.fold_in(seeds[6], part), 71), part)
    key_proj = draw_key_proj(jax.random.fold_in(jax.random.fold_in(seeds[6], part), 71), part)
    value = noise(part_splits[2], (TOKENS, WIDTH), 1.0, 6.0, ((0, 8), (1, 2)))
    block_mask = draw_block_mask(jax.random.fold_in(seeds[6], 71), part)
    tile_sizes = jax.vmap(lambda own: ragged_sizes(own, N_FRAMES, HALF, TILE_MAX, 2))(jax.random.split(seeds[4], N_REP)).reshape((N_REP, N_FRAMES)).astype(jnp.int32)
    temporal_ids = draw_temporal_ids(jax.random.fold_in(seeds[6], 71), part)
    return {"query": query, "key_proj": key_proj, "value": value, "block_mask": block_mask, "tile_sizes": tile_sizes, "temporal_ids": temporal_ids}


MASKED_SCORE = -1e30


def softmax_weights(scores):
    highest = jnp.max(scores, axis=-1, keepdims=True)
    raised = jnp.exp(scores - highest)
    return (raised / jnp.sum(raised, axis=-1, keepdims=True)).astype(jnp.bfloat16)


def reference(query, key_proj, value, block_mask, tile_sizes, temporal_ids):
    score_scale = HD ** -0.5

    def by_heads(array):
        return array.reshape(N_FRAMES, FRAME, HEADS, HD).transpose(2, 0, 1, 3)

    head_query = by_heads(query)
    head_keys = by_heads(key_proj)
    head_values = by_heads(value)

    def spatial_head(head_args):
        one_query, one_keys, one_values, one_mask = head_args
        scores = jnp.einsum("fad,fbd->fab", one_query.astype(jnp.float32), one_keys.astype(jnp.float32)) * score_scale
        allowed = jnp.repeat(jnp.repeat(one_mask, BLK, axis=0), BLK, axis=1) == 1
        scores = jnp.where(allowed[None], scores, MASKED_SCORE)
        weights = softmax_weights(scores)
        return jnp.einsum("fab,fbd->fad", weights.astype(jnp.float32), one_values.astype(jnp.float32)).astype(jnp.bfloat16)

    spatial_out = lax.map(spatial_head, (head_query, head_keys, head_values, block_mask))

    temp_query = head_query[temporal_ids]
    temp_keys = head_keys[temporal_ids]
    temp_values = head_values[temporal_ids]
    temp_out = jnp.zeros((TEMP, N_FRAMES, FRAME, HD), jnp.bfloat16)
    slot_index = jnp.arange(TILE_MAX, dtype=jnp.int32)
    for half_index in range(N_REP):
        tile_len = tile_sizes[half_index].astype(jnp.int32)
        starts = jnp.cumsum(tile_len).astype(jnp.int32) - tile_len
        positions = half_index * HALF + starts[:, None] + slot_index[None, :]
        live_slots = slot_index[None, :] < tile_len[:, None]
        safe_rows = jnp.minimum(positions, FRAME - 1).astype(jnp.int32)

        def temporal_tile(tile_args):
            rows_here, live_here = tile_args
            tile_query = temp_query[:, :, rows_here, :].reshape(TEMP, N_FRAMES * TILE_MAX, HD)
            tile_keys = temp_keys[:, :, rows_here, :].reshape(TEMP, N_FRAMES * TILE_MAX, HD)
            tile_values = temp_values[:, :, rows_here, :].reshape(TEMP, N_FRAMES * TILE_MAX, HD)
            key_live = jnp.tile(live_here, N_FRAMES)
            scores = jnp.einsum("hqd,hkd->hqk", tile_query.astype(jnp.float32), tile_keys.astype(jnp.float32)) * score_scale
            scores = jnp.where(key_live[None, None, :], scores, MASKED_SCORE)
            weights = softmax_weights(scores)
            tile_out = jnp.einsum("hqk,hkd->hqd", weights.astype(jnp.float32), tile_values.astype(jnp.float32)).astype(jnp.bfloat16)
            return tile_out.reshape(TEMP, N_FRAMES, TILE_MAX, HD)

        tile_out = lax.map(temporal_tile, (safe_rows, live_slots))
        target = jnp.where(live_slots, positions, FRAME).reshape(-1).astype(jnp.int32)
        placed = tile_out.transpose(1, 2, 0, 3, 4).reshape(TEMP, N_FRAMES, N_FRAMES * TILE_MAX, HD)
        temp_out = temp_out.at[:, :, target, :].set(placed, mode="drop")

    all_out = spatial_out.at[temporal_ids].set(temp_out)
    return all_out.transpose(1, 2, 0, 3).reshape(TOKENS, WIDTH)
```

```python
import functools
import math

import jax
import jax.numpy as jnp
from jax import lax
from jax.experimental import pallas as pl
from jax.experimental.pallas import tpu as pltpu
from jax.sharding import PartitionSpec as P

HD = 128
BLK = 64
MASKED_SCORE = -1e30
EXP2_SCALE = HD ** (-0.5) * math.log2(math.e)
MESH = pl.DeviceIdType.MESH


def softmax_weights(scores):
    highest = jnp.max(scores, axis=-1, keepdims=True)
    raised = jnp.exp(scores - highest)
    return (raised / jnp.sum(raised, axis=-1, keepdims=True)).astype(jnp.bfloat16)


def tile_numbers(positions, ends):
    return sum((positions >= end).astype(jnp.int32) for end in ends)


def plain(query, key_proj, value, block_mask, tile_sizes, temporal_ids):
    rows, heads_here = query.shape[0], block_mask.shape[0]
    temp_here, frame_blocks = temporal_ids.shape[0], block_mask.shape[1]
    score_scale = HD ** (-0.5)
    local_ids = temporal_ids - lax.axis_index("heads") * heads_here
    pick = local_ids[:, None] == jnp.arange(heads_here, dtype=jnp.int32)[None, :]

    def grid(rows_of):
        return rows_of.reshape(rows_of.shape[0], heads_here, HD)

    def chosen(rows_of):
        return jnp.einsum(
            "rhd,th->rtd", grid(rows_of), pick.astype(jnp.bfloat16), preferred_element_type=jnp.float32
        ).astype(jnp.bfloat16)

    temp_query = chosen(query)
    temp_keys = lax.all_gather(chosen(key_proj), "frames", axis=0, tiled=True)
    temp_values = lax.all_gather(chosen(value), "frames", axis=0, tiled=True)
    tile_len = tile_sizes[0]
    index = jnp.arange(tile_len.shape[0], dtype=jnp.int32)
    ends = jnp.sum(jnp.where(index[None, :] <= index[:, None], tile_len[None, :], 0), axis=1)
    positions = jnp.arange(rows, dtype=jnp.int32)
    tile_of = jnp.sum((positions[:, None] >= ends[None, :]).astype(jnp.int32), axis=1)
    scores = (
        jnp.einsum("qhd,khd->hqk", temp_query, temp_keys, preferred_element_type=jnp.float32) * score_scale
    )
    shaped = scores.reshape(temp_here, rows, -1, rows)
    same = tile_of[:, None] == tile_of[None, :]
    shaped = jnp.where(same[None, :, None, :], shaped, MASKED_SCORE)
    weights = softmax_weights(shaped.reshape(scores.shape))
    temp_out = jnp.einsum(
        "hqk,khd->qhd", weights, temp_values, preferred_element_type=jnp.float32
    ).astype(jnp.bfloat16)

    keys = grid(lax.all_gather(key_proj, "rep", axis=0, tiled=True))
    values = grid(lax.all_gather(value, "rep", axis=0, tiled=True))
    query_blocks = rows // BLK
    mask_rows = lax.dynamic_slice_in_dim(block_mask, lax.axis_index("rep") * query_blocks, query_blocks, 1)
    scores = jnp.einsum("qhd,khd->hqk", grid(query), keys, preferred_element_type=jnp.float32) * score_scale
    shaped = scores.reshape(heads_here, query_blocks, BLK, frame_blocks, BLK)
    shaped = jnp.where(mask_rows[:, :, None, :, None] == 1, shaped, MASKED_SCORE)
    weights = softmax_weights(shaped.reshape(scores.shape))
    spat_out = jnp.einsum("hqk,khd->qhd", weights, values, preferred_element_type=jnp.float32)
    spread = jnp.einsum(
        "rtd,th->rhd", temp_out, pick.astype(jnp.bfloat16), preferred_element_type=jnp.float32
    )
    is_temp = jnp.any(pick, axis=0)
    combined = jnp.where(is_temp[None, :, None], spread, spat_out)
    return combined.astype(jnp.bfloat16).reshape(rows, heads_here * HD)


def across(me, step):
    if step == 0:
        return me
    if step == 1:
        return me + 1 - 2 * lax.rem(me, 2)
    if step == 2:
        return lax.rem(me + 2, 4)
    return 3 - me


def weigh(scores, values):
    highest = jnp.max(scores, axis=-1, keepdims=True)
    raised = jnp.exp2(scores - highest)
    total = jnp.sum(raised, axis=-1, keepdims=True)
    out = jnp.dot(raised.astype(jnp.bfloat16), values, preferred_element_type=jnp.float32)
    return (out / total).astype(jnp.bfloat16)


def products(left, right):
    return lax.dot_general(left, right, (((1,), (1,)), ((), ())), preferred_element_type=jnp.float32)


def kernel(
    heads, ids, tiles, mask, q_hbm, k_hbm, v_hbm, out,
    q_own, k_own, v_own, q_heads, k_heads, v_heads, k_peer, v_peer, q_send, k_send, v_send, q_tile, k_tile, v_tile, o_send,
    held, mask_rows, tile_bias, load_sem, pair_send, pair_recv, z_send, z_recv,
):
    rows = q_own.shape[0]
    frames = 4
    blocks = rows // BLK
    me, half = lax.axis_index("frames"), lax.axis_index("rep")
    loads = [
        pltpu.make_async_copy(src, dst, load_sem.at[i])
        for i, (src, dst) in enumerate(((k_hbm, k_own), (v_hbm, v_own), (q_hbm, q_own)))
    ]
    for load in loads:
        load.start()
    barrier = pltpu.get_barrier_semaphore()
    for step in (1, 2, 3):
        pl.semaphore_signal(barrier, inc=1, device_id={"frames": across(me, step)}, device_id_type=MESH)
    pl.semaphore_signal(barrier, inc=1, device_id={"rep": 1 - half}, device_id_type=MESH)
    local_ids = [lax.rem(ids[across(me, step)], heads) for step in range(frames)]

    def pick(source, by_head, own_tile, sends):
        for h in range(heads):
            by_head[h] = source[:, h * HD : (h + 1) * HD]
        for step in (2, 3, 1, 0):
            if step:
                sends[step] = by_head[local_ids[step]]
            else:
                own_tile[pl.ds(0, rows), :] = by_head[local_ids[step]]

    def z_copy(kind, step, src, dst):
        return pltpu.make_async_remote_copy(
            src_ref=src, dst_ref=dst, send_sem=z_send.at[kind, step], recv_sem=z_recv.at[kind, step],
            device_id={"frames": across(me, step)}, device_id_type=MESH,
        )

    def pair_copy(i, src, dst):
        return pltpu.make_async_remote_copy(
            src_ref=src, dst_ref=dst, send_sem=pair_send.at[i], recv_sem=pair_recv.at[i],
            device_id={"rep": 1 - half}, device_id_type=MESH,
        )

    pairs = [pair_copy(0, k_hbm, k_peer), pair_copy(1, v_hbm, v_peer)]
    sent = []
    for kind, (source, by_head, own_tile, sends) in enumerate(
        ((k_own, k_heads, k_tile, k_send), (v_own, v_heads, v_tile, v_send), (q_own, q_heads, q_tile, q_send))
    ):
        loads[kind].wait()
        pick(source, by_head, own_tile, sends)
        if kind == 0:
            pl.semaphore_wait(barrier, frames)
        for step in (2, 3, 1):
            copy = z_copy(kind, step, sends.at[step], own_tile.at[pl.ds(step * rows, rows)])
            copy.start()
            sent.append(copy)
        if kind < 2:
            pairs[kind].start()

    ends, end = [], 0
    for j in range(frames):
        end = end + tiles[0, j]
        ends.append(end)
    down = lax.broadcasted_iota(jnp.int32, (rows, rows), 0)
    along = lax.broadcasted_iota(jnp.int32, (rows, rows), 1)
    tile_bias[...] = jnp.where(tile_numbers(down, ends) == tile_numbers(along, ends), 0.0, MASKED_SCORE)

    key_block = lax.rem(lax.broadcasted_iota(jnp.int32, (2 * blocks, 2 * rows), 1) // BLK + blocks * half, 2 * blocks)
    lies = (key_block == lax.broadcasted_iota(jnp.int32, (2 * blocks, 2 * rows), 0)).astype(jnp.bfloat16)
    flat_mask = mask[...].reshape(heads * 2 * blocks, 2 * blocks).astype(jnp.float32).astype(jnp.bfloat16)
    seen = jnp.dot(flat_mask, lies, preferred_element_type=jnp.float32)
    mask_rows[...] = jnp.where(seen > 0.5, 0.0, MASKED_SCORE)

    for pair in pairs:
        pair.wait()

    def spatial(h, carry):
        columns = pl.ds(pl.multiple_of(h * HD, HD), HD)
        bias = mask_rows[pl.ds(pl.multiple_of(h * 2 * blocks, 2 * blocks), 2 * blocks), :]
        bias = jnp.where(half == 0, bias[:blocks], bias[blocks:])
        bias = jnp.concatenate(
            [jnp.broadcast_to(bias[i : i + 1], (BLK, 2 * rows)) for i in range(blocks)], axis=0
        )
        q = q_heads[h]
        scores = jnp.concatenate(
            [products(q, k_heads[h]), products(q, k_peer[:, columns])], axis=1
        )
        values = jnp.concatenate([v_heads[h], v_peer[:, columns]], axis=0)
        held[h] = weigh(scores * EXP2_SCALE + bias, values)
        return carry

    lax.fori_loop(0, heads, spatial, 0)

    for copy in sent[:6]:
        copy.wait()
    returned = []
    for step in (2, 3, 1, 0):
        if step:
            sent[6 + (2, 3, 1).index(step)].wait()
        scores = products(q_tile[pl.ds(step * rows, rows), :], k_tile[...]) * EXP2_SCALE
        bias = jnp.concatenate([tile_bias[...]] * frames, axis=1)
        result = weigh(scores + bias, v_tile[...])
        if step:
            o_send[step] = result
            copy = z_copy(3, step, o_send.at[step], held.at[heads + step])
            copy.start()
            returned.append(copy)
        else:
            held[heads] = result
    for copy in returned:
        copy.wait()
    for h in range(heads):
        slot = h
        for step in range(frames):
            slot = jnp.where(local_ids[step] == h, heads + step, slot)
        out[:, h * HD : (h + 1) * HD] = held[slot]


def fused(query, key_proj, value, block_mask, tile_sizes, temporal_ids):
    rows, width = query.shape
    heads = block_mask.shape[0]
    whole = pltpu.VMEM((rows, width), jnp.bfloat16)
    parted = pltpu.VMEM((heads, rows, HD), jnp.bfloat16)
    tiles = pltpu.VMEM((4, rows, HD), jnp.bfloat16)
    flat = pltpu.VMEM((4 * rows, HD), jnp.bfloat16)
    smem, vmem = pl.BlockSpec(memory_space=pltpu.SMEM), pl.BlockSpec(memory_space=pltpu.VMEM)
    anywhere = pl.BlockSpec(memory_space=pl.ANY)
    return pl.pallas_call(
        functools.partial(kernel, heads),
        out_shape=jax.ShapeDtypeStruct((rows, width), jnp.bfloat16),
        in_specs=[smem, smem, vmem, anywhere, anywhere, anywhere],
        out_specs=vmem,
        scratch_shapes=[
            whole, whole, whole, parted, parted, parted, whole, whole, tiles, tiles, tiles, flat, flat, flat, tiles,
            pltpu.VMEM((heads + 4, rows, HD), jnp.bfloat16),
            pltpu.VMEM((heads * 2 * rows // BLK, 2 * rows), jnp.float32),
            pltpu.VMEM((rows, rows), jnp.float32),
            pltpu.SemaphoreType.DMA((3,)),
            pltpu.SemaphoreType.DMA((2,)),
            pltpu.SemaphoreType.DMA((2,)),
            pltpu.SemaphoreType.DMA((4, 4)),
            pltpu.SemaphoreType.DMA((4, 4)),
        ],
        compiler_params=pltpu.CompilerParams(
            collective_id=0, has_side_effects=True, vmem_limit_bytes=40 * 2**20
        ),
    )(temporal_ids, tile_sizes, block_mask, query, key_proj, value)


def solution(mesh):
    def local(query, key_proj, value, block_mask, tile_sizes, temporal_ids):
        by_head = mesh.shape["frames"] == temporal_ids.shape[0] == 4 and mesh.shape["rep"] == 2
        chosen = fused if by_head else plain
        return chosen(query, key_proj, value, block_mask, tile_sizes, temporal_ids)

    in_specs = (
        P(("groups", "frames", "rep"), "heads"),
        P(("groups", "frames", "rep"), "heads"),
        P(("groups", "frames", "rep"), "heads"),
        P("heads", None, None),
        P("rep", None),
        P("heads"),
    )
    out_specs = P(("groups", "frames", "rep"), "heads")
    return jax.shard_map(local, mesh=mesh, in_specs=in_specs, out_specs=out_specs, check_vma=False)
```

```python
import functools
import math

import jax
import jax.numpy as jnp
from jax import lax
from jax.experimental import pallas as pl
from jax.experimental.pallas import tpu as pltpu
from jax.sharding import PartitionSpec as P

HD = 128
BLK = 64
MASKED_SCORE = -1e30
EXP2_SCALE = HD ** (-0.5) * math.log2(math.e)
MESH = pl.DeviceIdType.MESH


def softmax_weights(scores):
    highest = jnp.max(scores, axis=-1, keepdims=True)
    raised = jnp.exp(scores - highest)
    return (raised / jnp.sum(raised, axis=-1, keepdims=True)).astype(jnp.bfloat16)


def tile_numbers(positions, ends):
    return sum((positions >= end).astype(jnp.int32) for end in ends)


def plain(query, key_proj, value, block_mask, tile_sizes, temporal_ids):
    rows, heads_here = query.shape[0], block_mask.shape[0]
    temp_here, frame_blocks = temporal_ids.shape[0], block_mask.shape[1]
    score_scale = HD ** (-0.5)
    local_ids = temporal_ids - lax.axis_index("heads") * heads_here
    pick = local_ids[:, None] == jnp.arange(heads_here, dtype=jnp.int32)[None, :]

    def grid(rows_of):
        return rows_of.reshape(rows_of.shape[0], heads_here, HD)

    def chosen(rows_of):
        return jnp.einsum(
            "rhd,th->rtd", grid(rows_of), pick.astype(jnp.bfloat16), preferred_element_type=jnp.float32
        ).astype(jnp.bfloat16)

    temp_query = chosen(query)
    temp_keys = lax.all_gather(chosen(key_proj), "frames", axis=0, tiled=True)
    temp_values = lax.all_gather(chosen(value), "frames", axis=0, tiled=True)
    tile_len = tile_sizes[0]
    index = jnp.arange(tile_len.shape[0], dtype=jnp.int32)
    ends = jnp.sum(jnp.where(index[None, :] <= index[:, None], tile_len[None, :], 0), axis=1)
    positions = jnp.arange(rows, dtype=jnp.int32)
    tile_of = jnp.sum((positions[:, None] >= ends[None, :]).astype(jnp.int32), axis=1)
    scores = (
        jnp.einsum("qhd,khd->hqk", temp_query, temp_keys, preferred_element_type=jnp.float32) * score_scale
    )
    shaped = scores.reshape(temp_here, rows, -1, rows)
    same = tile_of[:, None] == tile_of[None, :]
    shaped = jnp.where(same[None, :, None, :], shaped, MASKED_SCORE)
    weights = softmax_weights(shaped.reshape(scores.shape))
    temp_out = jnp.einsum(
        "hqk,khd->qhd", weights, temp_values, preferred_element_type=jnp.float32
    ).astype(jnp.bfloat16)

    keys = grid(lax.all_gather(key_proj, "rep", axis=0, tiled=True))
    values = grid(lax.all_gather(value, "rep", axis=0, tiled=True))
    query_blocks = rows // BLK
    mask_rows = lax.dynamic_slice_in_dim(block_mask, lax.axis_index("rep") * query_blocks, query_blocks, 1)
    scores = jnp.einsum("qhd,khd->hqk", grid(query), keys, preferred_element_type=jnp.float32) * score_scale
    shaped = scores.reshape(heads_here, query_blocks, BLK, frame_blocks, BLK)
    shaped = jnp.where(mask_rows[:, :, None, :, None] == 1, shaped, MASKED_SCORE)
    weights = softmax_weights(shaped.reshape(scores.shape))
    spat_out = jnp.einsum("hqk,khd->qhd", weights, values, preferred_element_type=jnp.float32)
    spread = jnp.einsum(
        "rtd,th->rhd", temp_out, pick.astype(jnp.bfloat16), preferred_element_type=jnp.float32
    )
    is_temp = jnp.any(pick, axis=0)
    combined = jnp.where(is_temp[None, :, None], spread, spat_out)
    return combined.astype(jnp.bfloat16).reshape(rows, heads_here * HD)


def across(me, step):
    if step == 0:
        return me
    if step == 1:
        return me + 1 - 2 * lax.rem(me, 2)
    if step == 2:
        return lax.rem(me + 2, 4)
    return 3 - me


def weigh(scores, values):
    highest = jnp.max(scores, axis=-1, keepdims=True)
    raised = jnp.exp2(scores - highest)
    total = jnp.sum(raised, axis=-1, keepdims=True)
    out = jnp.dot(raised.astype(jnp.bfloat16), values, preferred_element_type=jnp.float32)
    return (out / total).astype(jnp.bfloat16)


def products(left, right):
    return lax.dot_general(left, right, (((1,), (1,)), ((), ())), preferred_element_type=jnp.float32)


def kernel(
    heads, ids_hbm, tiles_hbm, mask_hbm, q_hbm, k_hbm, v_hbm, out, ids, tiles, mask,
    q_own, k_own, v_own, q_heads, k_heads, v_heads, k_peer, v_peer, q_send, k_send, v_send, q_tile, k_tile, v_tile, o_send,
    held, mask_rows, tile_bias, load_sem, pair_send, pair_recv, z_send, z_recv,
):
    rows = q_own.shape[0]
    frames = 4
    blocks = rows // BLK
    me, half = lax.axis_index("frames"), lax.axis_index("rep")
    loads = [
        pltpu.make_async_copy(src, dst, load_sem.at[i])
        for i, (src, dst) in enumerate(
            ((k_hbm, k_own), (v_hbm, v_own), (q_hbm, q_own), (ids_hbm, ids), (tiles_hbm, tiles), (mask_hbm, mask))
        )
    ]
    for i in (3, 0, 1, 2, 4, 5):
        loads[i].start()
    barrier = pltpu.get_barrier_semaphore()
    for step in (1, 2, 3):
        pl.semaphore_signal(barrier, inc=1, device_id={"frames": across(me, step)}, device_id_type=MESH)
    pl.semaphore_signal(barrier, inc=1, device_id={"rep": 1 - half}, device_id_type=MESH)
    loads[3].wait()
    local_ids = [lax.rem(ids[across(me, step)], heads) for step in range(frames)]

    def pick(source, by_head, own_tile, sends):
        for h in range(heads):
            by_head[h] = source[:, h * HD : (h + 1) * HD]
        for step in (2, 3, 1, 0):
            if step:
                sends[step] = by_head[local_ids[step]]
            else:
                own_tile[pl.ds(0, rows), :] = by_head[local_ids[step]]

    def z_copy(kind, step, src, dst):
        return pltpu.make_async_remote_copy(
            src_ref=src, dst_ref=dst, send_sem=z_send.at[kind, step], recv_sem=z_recv.at[kind, step],
            device_id={"frames": across(me, step)}, device_id_type=MESH,
        )

    def pair_copy(i, src, dst):
        return pltpu.make_async_remote_copy(
            src_ref=src, dst_ref=dst, send_sem=pair_send.at[i], recv_sem=pair_recv.at[i],
            device_id={"rep": 1 - half}, device_id_type=MESH,
        )

    pairs = [pair_copy(0, k_hbm, k_peer), pair_copy(1, v_hbm, v_peer)]
    sent = {}
    for kind, (source, by_head, own_tile, sends) in enumerate(
        ((k_own, k_heads, k_tile, k_send), (v_own, v_heads, v_tile, v_send), (q_own, q_heads, q_tile, q_send))
    ):
        loads[kind].wait()
        pick(source, by_head, own_tile, sends)
        if kind == 0:
            pl.semaphore_wait(barrier, frames)
        for step in (2, 3, 1):
            copy = z_copy(kind, step, sends.at[step], own_tile.at[pl.ds(step * rows, rows)])
            copy.start()
            sent[kind, step] = copy
        if kind < 2:
            pairs[kind].start()

    loads[4].wait()
    loads[5].wait()
    ends, end = [], 0
    for j in range(frames):
        end = end + tiles[0, j]
        ends.append(end)
    down = lax.broadcasted_iota(jnp.int32, (rows, rows), 0)
    along = lax.broadcasted_iota(jnp.int32, (rows, rows), 1)
    tile_bias[...] = jnp.where(tile_numbers(down, ends) == tile_numbers(along, ends), 0.0, MASKED_SCORE)

    key_block = lax.rem(lax.broadcasted_iota(jnp.int32, (2 * blocks, 2 * rows), 1) // BLK + blocks * half, 2 * blocks)
    lies = (key_block == lax.broadcasted_iota(jnp.int32, (2 * blocks, 2 * rows), 0)).astype(jnp.float32)
    for i in range(blocks):
        seen = lax.dot_general(
            mask[half * blocks + i].astype(jnp.float32), lies, (((0,), (0,)), ((), ())),
            preferred_element_type=jnp.float32,
        )
        mask_rows[i] = jnp.where(seen > 0.5, 0.0, MASKED_SCORE)

    for pair in pairs:
        pair.wait()

    def spatial(h, carry):
        columns = pl.ds(pl.multiple_of(h * HD, HD), HD)
        bias = jnp.concatenate(
            [jnp.broadcast_to(mask_rows[i, pl.ds(h, 1), :], (BLK, 2 * rows)) for i in range(blocks)], axis=0
        )
        q = q_heads[h]
        scores = jnp.concatenate(
            [products(q, k_heads[h]), products(q, k_peer[:, columns])], axis=1
        )
        values = jnp.concatenate([v_heads[h], v_peer[:, columns]], axis=0)
        held[h] = weigh(scores * EXP2_SCALE + bias, values)
        return carry

    lax.fori_loop(0, heads, spatial, 0)

    for step in (2, 3, 1):
        sent[0, step].wait()
        sent[1, step].wait()
    returned = []
    for step in (2, 3, 1, 0):
        if step:
            sent[2, step].wait()
        scores = products(q_tile[pl.ds(step * rows, rows), :], k_tile[...]) * EXP2_SCALE
        bias = jnp.concatenate([tile_bias[...]] * frames, axis=1)
        result = weigh(scores + bias, v_tile[...])
        if step:
            o_send[step] = result
            copy = z_copy(3, step, o_send.at[step], held.at[heads + step])
            copy.start()
            returned.append(copy)
        else:
            held[heads] = result
    for copy in returned:
        copy.wait()
    for h in range(heads):
        slot = h
        for step in range(frames):
            slot = jnp.where(local_ids[step] == h, heads + step, slot)
        out[:, h * HD : (h + 1) * HD] = held[slot]


def fused(query, key_proj, value, block_mask, tile_sizes, temporal_ids):
    rows, width = query.shape
    heads = block_mask.shape[0]
    whole = pltpu.VMEM((rows, width), jnp.bfloat16)
    parted = pltpu.VMEM((heads, rows, HD), jnp.bfloat16)
    tiles = pltpu.VMEM((4, rows, HD), jnp.bfloat16)
    flat = pltpu.VMEM((4 * rows, HD), jnp.bfloat16)
    turned = block_mask.transpose(1, 2, 0)
    operands = (temporal_ids, tile_sizes, turned, query, key_proj, value)
    return pl.pallas_call(
        functools.partial(kernel, heads),
        out_shape=pltpu.VMEM((rows, width), jnp.bfloat16),
        in_specs=[pl.BlockSpec(memory_space=pltpu.HBM)] * len(operands),
        out_specs=pl.BlockSpec(memory_space=pltpu.VMEM),
        scratch_shapes=[
            pltpu.SMEM(temporal_ids.shape, jnp.int32),
            pltpu.SMEM(tile_sizes.shape, jnp.int32),
            pltpu.VMEM(turned.shape, jnp.int32),
            whole, whole, whole, parted, parted, parted, whole, whole, tiles, tiles, tiles, flat, flat, flat, tiles,
            pltpu.VMEM((heads + 4, rows, HD), jnp.bfloat16),
            pltpu.VMEM((rows // BLK, heads, 2 * rows), jnp.float32),
            pltpu.VMEM((rows, rows), jnp.float32),
            pltpu.SemaphoreType.DMA((6,)),
            pltpu.SemaphoreType.DMA((2,)),
            pltpu.SemaphoreType.DMA((2,)),
            pltpu.SemaphoreType.DMA((4, 4)),
            pltpu.SemaphoreType.DMA((4, 4)),
        ],
        compiler_params=pltpu.CompilerParams(
            collective_id=0, has_side_effects=True, vmem_limit_bytes=40 * 2**20
        ),
    )(*(pltpu.with_memory_space_constraint(x, pltpu.HBM) for x in operands))


def solution(mesh):
    def local(query, key_proj, value, block_mask, tile_sizes, temporal_ids):
        by_head = mesh.shape["frames"] == temporal_ids.shape[0] == 4 and mesh.shape["rep"] == 2
        chosen = fused if by_head else plain
        return chosen(query, key_proj, value, block_mask, tile_sizes, temporal_ids)

    in_specs = (
        P(("groups", "frames", "rep"), "heads"),
        P(("groups", "frames", "rep"), "heads"),
        P(("groups", "frames", "rep"), "heads"),
        P("heads", None, None),
        P("rep", None),
        P("heads"),
    )
    out_specs = P(("groups", "frames", "rep"), "heads")
    return jax.shard_map(local, mesh=mesh, in_specs=in_specs, out_specs=out_specs, check_vma=False)
```

```python
import functools
import math

import jax
import jax.numpy as jnp
from jax import lax
from jax.experimental import pallas as pl
from jax.experimental.pallas import tpu as pltpu
from jax.sharding import PartitionSpec as P

HD = 128
BLK = 64
MASKED_SCORE = -1e30
EXP2_SCALE = HD ** (-0.5) * math.log2(math.e)
MESH = pl.DeviceIdType.MESH


def softmax_weights(scores):
    highest = jnp.max(scores, axis=-1, keepdims=True)
    raised = jnp.exp(scores - highest)
    return (raised / jnp.sum(raised, axis=-1, keepdims=True)).astype(jnp.bfloat16)


def tile_numbers(positions, ends):
    return sum((positions >= end).astype(jnp.int32) for end in ends)


def plain(query, key_proj, value, block_mask, tile_sizes, temporal_ids):
    rows, heads_here = query.shape[0], block_mask.shape[0]
    temp_here, frame_blocks = temporal_ids.shape[0], block_mask.shape[1]
    score_scale = HD ** (-0.5)
    local_ids = temporal_ids - lax.axis_index("heads") * heads_here
    pick = local_ids[:, None] == jnp.arange(heads_here, dtype=jnp.int32)[None, :]

    def grid(rows_of):
        return rows_of.reshape(rows_of.shape[0], heads_here, HD)

    def chosen(rows_of):
        return jnp.einsum(
            "rhd,th->rtd", grid(rows_of), pick.astype(jnp.bfloat16), preferred_element_type=jnp.float32
        ).astype(jnp.bfloat16)

    temp_query = chosen(query)
    temp_keys = lax.all_gather(chosen(key_proj), "frames", axis=0, tiled=True)
    temp_values = lax.all_gather(chosen(value), "frames", axis=0, tiled=True)
    tile_len = tile_sizes[0]
    index = jnp.arange(tile_len.shape[0], dtype=jnp.int32)
    ends = jnp.sum(jnp.where(index[None, :] <= index[:, None], tile_len[None, :], 0), axis=1)
    positions = jnp.arange(rows, dtype=jnp.int32)
    tile_of = jnp.sum((positions[:, None] >= ends[None, :]).astype(jnp.int32), axis=1)
    scores = (
        jnp.einsum("qhd,khd->hqk", temp_query, temp_keys, preferred_element_type=jnp.float32) * score_scale
    )
    shaped = scores.reshape(temp_here, rows, -1, rows)
    same = tile_of[:, None] == tile_of[None, :]
    shaped = jnp.where(same[None, :, None, :], shaped, MASKED_SCORE)
    weights = softmax_weights(shaped.reshape(scores.shape))
    temp_out = jnp.einsum(
        "hqk,khd->qhd", weights, temp_values, preferred_element_type=jnp.float32
    ).astype(jnp.bfloat16)

    keys = grid(lax.all_gather(key_proj, "rep", axis=0, tiled=True))
    values = grid(lax.all_gather(value, "rep", axis=0, tiled=True))
    query_blocks = rows // BLK
    mask_rows = lax.dynamic_slice_in_dim(block_mask, lax.axis_index("rep") * query_blocks, query_blocks, 1)
    scores = jnp.einsum("qhd,khd->hqk", grid(query), keys, preferred_element_type=jnp.float32) * score_scale
    shaped = scores.reshape(heads_here, query_blocks, BLK, frame_blocks, BLK)
    shaped = jnp.where(mask_rows[:, :, None, :, None] == 1, shaped, MASKED_SCORE)
    weights = softmax_weights(shaped.reshape(scores.shape))
    spat_out = jnp.einsum("hqk,khd->qhd", weights, values, preferred_element_type=jnp.float32)
    spread = jnp.einsum(
        "rtd,th->rhd", temp_out, pick.astype(jnp.bfloat16), preferred_element_type=jnp.float32
    )
    is_temp = jnp.any(pick, axis=0)
    combined = jnp.where(is_temp[None, :, None], spread, spat_out)
    return combined.astype(jnp.bfloat16).reshape(rows, heads_here * HD)


def across(me, step):
    if step == 0:
        return me
    if step == 1:
        return me + 1 - 2 * lax.rem(me, 2)
    if step == 2:
        return lax.rem(me + 2, 4)
    return 3 - me


def weigh(scores, values):
    highest = jnp.max(scores, axis=-1, keepdims=True)
    raised = jnp.exp2(scores - highest)
    total = jnp.sum(raised, axis=-1, keepdims=True)
    out = jnp.dot(raised.astype(jnp.bfloat16), values, preferred_element_type=jnp.float32)
    return (out / total).astype(jnp.bfloat16)


def products(left, right):
    return lax.dot_general(left, right, (((1,), (1,)), ((), ())), preferred_element_type=jnp.float32)


def kernel(
    heads, ids_hbm, tiles_hbm, mask_hbm, q_hbm, k_hbm, v_hbm, out, ids, tiles, mask,
    q_own, k_own, v_own, q_heads, k_heads, v_heads, k_peer, v_peer, q_send, k_send, v_send, q_tile, k_tile, v_tile, o_send,
    held, mask_rows, tile_bias, load_sem, pair_send, pair_recv, z_send, z_recv,
):
    rows = q_own.shape[0]
    frames = 4
    blocks = rows // BLK
    me, half = lax.axis_index("frames"), lax.axis_index("rep")
    loads = [
        pltpu.make_async_copy(src, dst, load_sem.at[i])
        for i, (src, dst) in enumerate(
            ((k_hbm, k_own), (v_hbm, v_own), (q_hbm, q_own), (ids_hbm, ids), (tiles_hbm, tiles), (mask_hbm, mask))
        )
    ]
    side = heads // 2 * HD
    loads[0] = pltpu.make_async_copy(k_hbm.at[:, :side], k_own.at[:, :side], load_sem.at[0])
    later_keys = pltpu.make_async_copy(k_hbm.at[:, side:], k_own.at[:, side:], load_sem.at[6])
    loads[3].start()
    loads[0].start()
    later_keys.start()
    for i in (1, 2, 4, 5):
        loads[i].start()
    barrier = pltpu.get_barrier_semaphore()
    for step in (1, 2, 3):
        pl.semaphore_signal(barrier, inc=1, device_id={"frames": across(me, step)}, device_id_type=MESH)
    pl.semaphore_signal(barrier, inc=1, device_id={"rep": 1 - half}, device_id_type=MESH)
    loads[3].wait()
    local_ids = [lax.rem(ids[across(me, step)], heads) for step in range(frames)]

    def pick(source, by_head, own_tile, sends):
        for h in range(heads):
            if source is k_own and h == heads // 2:
                later_keys.wait()
            by_head[h] = source[:, h * HD : (h + 1) * HD]
        for step in (2, 3, 1, 0):
            if step:
                sends[step] = by_head[local_ids[step]]
            else:
                own_tile[pl.ds(0, rows), :] = by_head[local_ids[step]]

    def z_copy(kind, step, src, dst):
        return pltpu.make_async_remote_copy(
            src_ref=src, dst_ref=dst, send_sem=z_send.at[kind, step], recv_sem=z_recv.at[kind, step],
            device_id={"frames": across(me, step)}, device_id_type=MESH,
        )

    def pair_copy(i, src, dst):
        return pltpu.make_async_remote_copy(
            src_ref=src, dst_ref=dst, send_sem=pair_send.at[i], recv_sem=pair_recv.at[i],
            device_id={"rep": 1 - half}, device_id_type=MESH,
        )

    pairs = [pair_copy(0, k_hbm, k_peer), pair_copy(1, v_hbm, v_peer)]
    sent = {}
    for kind, (source, by_head, own_tile, sends) in enumerate(
        ((k_own, k_heads, k_tile, k_send), (v_own, v_heads, v_tile, v_send), (q_own, q_heads, q_tile, q_send))
    ):
        loads[kind].wait()
        pick(source, by_head, own_tile, sends)
        if kind == 0:
            pl.semaphore_wait(barrier, frames)
        for step in (2, 3, 1):
            copy = z_copy(kind, step, sends.at[step], own_tile.at[pl.ds(step * rows, rows)])
            copy.start()
            sent[kind, step] = copy
        if kind < 2:
            pairs[kind].start()

    loads[4].wait()
    loads[5].wait()
    ends, end = [], 0
    for j in range(frames):
        end = end + tiles[0, j]
        ends.append(end)
    down = lax.broadcasted_iota(jnp.int32, (rows, rows), 0)
    along = lax.broadcasted_iota(jnp.int32, (rows, rows), 1)
    tile_bias[...] = jnp.where(tile_numbers(down, ends) == tile_numbers(along, ends), 0.0, MASKED_SCORE)

    key_block = lax.rem(lax.broadcasted_iota(jnp.int32, (2 * blocks, 2 * rows), 1) // BLK + blocks * half, 2 * blocks)
    lies = (key_block == lax.broadcasted_iota(jnp.int32, (2 * blocks, 2 * rows), 0)).astype(jnp.float32)
    for i in range(blocks):
        seen = lax.dot_general(
            mask[half * blocks + i].astype(jnp.float32), lies, (((0,), (0,)), ((), ())),
            preferred_element_type=jnp.float32,
        )
        mask_rows[i] = jnp.where(seen > 0.5, 0.0, MASKED_SCORE)

    for pair in pairs:
        pair.wait()

    def spatial(h, carry):
        columns = pl.ds(pl.multiple_of(h * HD, HD), HD)
        bias = jnp.concatenate(
            [jnp.broadcast_to(mask_rows[i, pl.ds(h, 1), :], (BLK, 2 * rows)) for i in range(blocks)], axis=0
        )
        q = q_heads[h]
        scores = jnp.concatenate(
            [products(q, k_heads[h]), products(q, k_peer[:, columns])], axis=1
        )
        values = jnp.concatenate([v_heads[h], v_peer[:, columns]], axis=0)
        held[h] = weigh(scores * EXP2_SCALE + bias, values)
        return carry

    lax.fori_loop(0, heads, spatial, 0)

    for step in (2, 3, 1):
        sent[0, step].wait()
        sent[1, step].wait()
    returned = []
    for step in (2, 3, 1, 0):
        if step:
            sent[2, step].wait()
        scores = products(q_tile[pl.ds(step * rows, rows), :], k_tile[...]) * EXP2_SCALE
        bias = jnp.concatenate([tile_bias[...]] * frames, axis=1)
        result = weigh(scores + bias, v_tile[...])
        if step:
            o_send[step] = result
            copy = z_copy(3, step, o_send.at[step], held.at[heads + step])
            copy.start()
            returned.append(copy)
        else:
            held[heads] = result
    for copy in returned:
        copy.wait()
    for h in range(heads):
        slot = h
        for step in range(frames):
            slot = jnp.where(local_ids[step] == h, heads + step, slot)
        out[:, h * HD : (h + 1) * HD] = held[slot]


def fused(query, key_proj, value, block_mask, tile_sizes, temporal_ids):
    rows, width = query.shape
    heads = block_mask.shape[0]
    whole = pltpu.VMEM((rows, width), jnp.bfloat16)
    parted = pltpu.VMEM((heads, rows, HD), jnp.bfloat16)
    tiles = pltpu.VMEM((4, rows, HD), jnp.bfloat16)
    flat = pltpu.VMEM((4 * rows, HD), jnp.bfloat16)
    turned = block_mask.transpose(1, 2, 0)
    operands = (temporal_ids, tile_sizes, turned, query, key_proj, value)
    return pl.pallas_call(
        functools.partial(kernel, heads),
        out_shape=pltpu.VMEM((rows, width), jnp.bfloat16),
        in_specs=[pl.BlockSpec(memory_space=pltpu.HBM)] * len(operands),
        out_specs=pl.BlockSpec(memory_space=pltpu.VMEM),
        scratch_shapes=[
            pltpu.SMEM(temporal_ids.shape, jnp.int32),
            pltpu.SMEM(tile_sizes.shape, jnp.int32),
            pltpu.VMEM(turned.shape, jnp.int32),
            whole, whole, whole, parted, parted, parted, whole, whole, tiles, tiles, tiles, flat, flat, flat, tiles,
            pltpu.VMEM((heads + 4, rows, HD), jnp.bfloat16),
            pltpu.VMEM((rows // BLK, heads, 2 * rows), jnp.float32),
            pltpu.VMEM((rows, rows), jnp.float32),
            pltpu.SemaphoreType.DMA((7,)),
            pltpu.SemaphoreType.DMA((2,)),
            pltpu.SemaphoreType.DMA((2,)),
            pltpu.SemaphoreType.DMA((4, 4)),
            pltpu.SemaphoreType.DMA((4, 4)),
        ],
        compiler_params=pltpu.CompilerParams(
            collective_id=0, has_side_effects=True, vmem_limit_bytes=40 * 2**20
        ),
    )(*(pltpu.with_memory_space_constraint(x, pltpu.HBM) for x in operands))


def solution(mesh):
    def local(query, key_proj, value, block_mask, tile_sizes, temporal_ids):
        by_head = mesh.shape["frames"] == temporal_ids.shape[0] == 4 and mesh.shape["rep"] == 2
        chosen = fused if by_head else plain
        return chosen(query, key_proj, value, block_mask, tile_sizes, temporal_ids)

    in_specs = (
        P(("groups", "frames", "rep"), "heads"),
        P(("groups", "frames", "rep"), "heads"),
        P(("groups", "frames", "rep"), "heads"),
        P("heads", None, None),
        P("rep", None),
        P("heads"),
    )
    out_specs = P(("groups", "frames", "rep"), "heads")
    return jax.shard_map(local, mesh=mesh, in_specs=in_specs, out_specs=out_specs, check_vma=False)
```
